32 devices in a mesh: groups: 1, wide: 32 (over z, y, x, core).
Axes of the slice: x: 2, y: 2, z: 4, core: 2. Of those that a mesh axis runs over, the one named last changes fastest.
Arguments:
- inputs: bfloat16 [3, 128, 8192], P(None, 'groups', 'wide'), may hold values from -6 to 6
- base_weight: bfloat16 [8192, 8192], P('wide'), may hold values from -0.0625 to 0.0625
- shrink_table: bfloat16 [64, 64, 8192], P('wide'), may hold values from -0.0625 to 0.0625
- expand_table: bfloat16 [64, 64, 8192], P('wide'), may hold values from -0.75 to 0.75
- table_slot: int32 [64], replicated, may hold values from 0 to 63, each once
- adapter_ids: int32 [3, 128], P(None, 'groups'), may hold values from 0 to 63
Outputs:
- projected: bfloat16 [3, 128, 8192], P(None, 'groups', 'wide')
The draws below stay inside these ranges and needn't reach their ends.
Inputs may be any that keep to these rules, and one draw needn't show every extreme that they name: `table_slot`: each table row holds exactly one adapter; table rows t * 2 to (t + 1) * 2 - 1 stand on index t of wide.
All inputs are finite; a program needn't handle non-finite values.
Results may differ from the reference program's by a relative error of at most 0.0048.
Values may be sent and summed in bfloat16 or wider, within the bound.
No kernel may reach another device: no remote copies, remote signals or barrier semaphores. Data moves between devices by JAX's collectives and lax.ppermute only.
A program may use at most 128 MiB of HBM per device.

```python
import math
import jax
import jax.numpy as jnp
import numpy as np
from jax import lax

D = 8192
RANK = 64
REQ_DEV = 4
STEPS = 3
REQUESTS = 128
NADAPT = 64
N_WIDE = 32


def plant(result, rng, smallest, top_value):
    shape = result.shape
    place = [jax.random.randint(jax.random.fold_in(rng, axis), (), 0, shape[axis]) for axis in range(len(shape))]
    result = result.at[tuple(place)].set(smallest)
    longest = shape.index(max(shape))
    place[longest] = (place[longest] + 1) % shape[longest]
    return result.at[tuple(place)].set(top_value)


def shard_levels(own_key, dims, shards, least, largest):
    gain, own = 1.0, jax.random.fold_in(own_key, 6)
    for dim, blocks in shards:
        steps = jnp.exp(jax.random.uniform(jax.random.fold_in(own, dim), (blocks,), jnp.float32, least / len(shards), largest / len(shards)))
        gain = gain * jnp.repeat(steps, dims[dim] // blocks).reshape([-1 if axis == dim else 1 for axis in range(len(dims))])
    return gain


def rank_table(number_of, slope):
    weights = [(1 << 20) // math.isqrt(rank ** slope) + 1 for rank in range(1, number_of + 1)]
    width = 1 + sum(weights) // (1 << 30)
    return np.cumsum(np.array([max(1, weight // width) for weight in weights]))


def ranked_ids(key, dims, number_of, skew):
    grid = rank_table(number_of, skew)
    pick = jax.random.randint(jax.random.fold_in(key, 1), dims, 0, int(grid[number_of - 1]))
    grade = jnp.searchsorted(jnp.asarray(grid, jnp.int32), pick, side="right")
    return jax.random.permutation(jax.random.fold_in(key, 2), number_of)[grade].astype(jnp.int32)


def gaussian(rng, extent, deviation, most, pieces=(), dtype=jnp.bfloat16):
    level = shard_levels(rng, extent, pieces, -0.22, 0.18) if pieces else 1.0
    entries = jax.random.normal(rng, extent, jnp.float32) * deviation * level
    return jnp.minimum(jnp.maximum(entries, -most), most).astype(dtype)


def setup_inputs(seed: int = 0, part: int = 0) -> dict:
    seeds = jax.random.split(jax.random.key(seed), 7)
    part_keys = jax.random.split(jax.random.fold_in(seeds[6], part), 7)
    return {
        "inputs": gaussian(part_keys[0], (STEPS, REQUESTS, D), 1.0, 6.0, ((2, 32),)),
        "base_weight": gaussian(seeds[1], (D, D), D ** -0.5, 0.0625, ((0, 32),)),
        "shrink_table": gaussian(seeds[2], (NADAPT, RANK, D), D ** -0.5, 0.0625, ((0, 32),)),
        "expand_table": gaussian(seeds[3], (NADAPT, RANK, D), RANK ** -0.5, 0.75, ((0, 32),)),
        "table_slot": jax.random.permutation(seeds[4], NADAPT).astype(jnp.int32),
        "adapter_ids": plant(ranked_ids(part_keys[5], (STEPS, REQUESTS), NADAPT, 1), jax.random.fold_in(part_keys[5], 3), 0, NADAPT - 1).astype(jnp.int32),
    }


def reference(inputs, base_weight, shrink_table, expand_table, table_slot, adapter_ids):
    slot_rows = table_slot[adapter_ids].astype(jnp.int32)
    results = []
    for step_index in range(STEPS):
        base_out = jnp.dot(inputs[step_index], base_weight.T, preferred_element_type=jnp.float32)

        def apply_block(operands):
            block_rows, block_slots = operands
            shrink_rows = shrink_table[block_slots].astype(jnp.float32)
            shrink = jnp.einsum("rd,rkd->rk", block_rows.astype(jnp.float32), shrink_rows)
            low_rank = lax.optimization_barrier(shrink.astype(jnp.bfloat16)).astype(jnp.float32)
            expand_rows = expand_table[block_slots].astype(jnp.float32)
            return jnp.einsum("rko,rk->ro", expand_rows, low_rank)

        adapter_out = lax.map(apply_block, (inputs[step_index].reshape(N_WIDE, REQ_DEV, D), slot_rows[step_index].reshape(N_WIDE, REQ_DEV)))
        adapter_out = adapter_out.reshape(REQ_DEV * N_WIDE, D)
        results.append((base_out + 2.0 * adapter_out).astype(jnp.bfloat16))
    return jnp.stack(results)
```

```python
import functools

import jax
import jax.numpy as jnp
from jax import lax
from jax.experimental import pallas as pl
from jax.experimental.pallas import tpu as pltpu
from jax.sharding import PartitionSpec as P

SLOTS = 32
NT = (((1,), (1,)), ((), ()))
F32 = jnp.float32
BF16 = jnp.bfloat16


def vmem(count):
    return [pl.BlockSpec(memory_space=pltpu.VMEM)] * count


def owner_kernel(rows_ref, mask_ref, s0_ref, s1_ref, e0_ref, e1_ref, out_ref):
    parts, _, width = rows_ref.shape
    half = s0_ref.shape[0]
    lows = []
    for index, table in enumerate((s0_ref, s1_ref)):
        total = jnp.zeros((rows_ref.shape[1], half), F32)
        for part in range(parts):
            total += lax.dot_general(
                rows_ref[part], table[:, part * width : (part + 1) * width], NT, preferred_element_type=F32
            )
        lows.append((total * mask_ref[:, index * half : (index + 1) * half]).astype(BF16))
    for part in range(parts):
        columns = slice(part * width, (part + 1) * width)
        value = jnp.dot(lows[0], e0_ref[:, columns], preferred_element_type=F32)
        value += jnp.dot(lows[1], e1_ref[:, columns], preferred_element_type=F32)
        out_ref[part] = value.astype(BF16)


def owner(rows, mask, s0, s1, e0, e1):
    return pl.pallas_call(
        owner_kernel,
        out_shape=jax.ShapeDtypeStruct(rows.shape, BF16),
        in_specs=vmem(6),
        out_specs=vmem(1)[0],
        compiler_params=pltpu.CompilerParams(vmem_limit_bytes=32 << 20),
        name="owner",
    )(rows, mask, s0, s1, e0, e1)


def base_kernel(whole, place_ref, *refs):
    *blocks, w0_ref, w1_ref, out0_ref, out1_ref = refs
    rows = out0_ref.shape[0]
    width = blocks[0].shape[1] // 2
    for w_ref, out_ref in ((w0_ref, out0_ref), (w1_ref, out1_ref)):
        total = jnp.zeros(out_ref.shape, F32)
        for part in range(len(whole)):
            first = whole[part]
            block = blocks[first][...]
            if block.shape[0] != rows:
                block = jnp.concatenate([block, blocks[first + 1][...]], axis=0)
            for side in range(2):
                start = pl.multiple_of(place_ref[2 * part + side], width)
                total += lax.dot_general(
                    block[:, side * width : (side + 1) * width],
                    w_ref[:, pl.ds(start, width)],
                    NT,
                    preferred_element_type=F32,
                )
        out_ref[...] = total


def base(places, blocks, whole, w0, w1):
    rows = blocks[0].shape[0]
    shape = jax.ShapeDtypeStruct((rows, w0.shape[0]), F32)
    return pl.pallas_call(
        functools.partial(base_kernel, whole),
        out_shape=(shape, shape),
        in_specs=[pl.BlockSpec(memory_space=pltpu.SMEM)] + vmem(len(blocks) + 2),
        out_specs=tuple(vmem(2)),
        compiler_params=pltpu.CompilerParams(vmem_limit_bytes=40 << 20),
        name="base",
    )(places, *blocks, w0, w1)


def body(groups, inputs, base_weight, shrink_table, expand_table, table_slot, adapter_ids):
    wide = lax.axis_size("wide")
    me = lax.axis_index("wide")
    core, chip = me % 2, me // 2
    chips = wide // 2
    steps, requests, width = inputs.shape
    count = steps * requests
    held, rank, _ = shrink_table.shape
    features = inputs.reshape(count, width)

    def move(value, target):
        pairs = [(2 * c + k, 2 * target(c) + k) for c in range(chips) for k in range(2)]
        return lax.ppermute(value, "wide", pairs)

    def swap(value):
        return lax.ppermute(value, "wide", [(i, i ^ 1) for i in range(wide)])

    def flip(bits):
        return lambda c: c ^ bits

    def shift(k):
        return lambda c: (c + 4 * k) % chips

    half = requests // 2
    split = inputs.reshape(steps, 2, half, width)
    own_half = lax.dynamic_index_in_dim(split, core, 1, keepdims=False).reshape(steps * half, width)
    other_half = lax.dynamic_index_in_dim(split, 1 - core, 1, keepdims=False).reshape(steps * half, width)
    block = jnp.concatenate([own_half, swap(other_half)], axis=1)

    table = table_slot.shape[0]
    ids = adapter_ids.reshape(count)
    slot = jnp.sum((ids[:, None] == jnp.arange(table, dtype=jnp.int32)) * table_slot, axis=1)
    holder = slot // (2 * held)
    earlier = jnp.arange(count)[:, None] > jnp.arange(count)
    order = jnp.sum((holder[:, None] == holder) & earlier, axis=1)
    local = (slot - me // 2 * (2 * held) - core * held) % (2 * held)
    per_chip = 2 * SLOTS

    shrink0 = shrink_table.reshape(held * rank, -1)
    expand0 = expand_table.reshape(held * rank, -1)
    shrink1, expand1 = swap(shrink0), swap(expand0)

    def exchange(value):
        return lax.all_to_all(value, "wide", split_axis=0, concat_axis=0, tiled=True)

    def round_of(index):
        rest = order - index * per_chip
        place = jnp.where((rest >= 0) & (rest < per_chip), holder * per_chip + rest, -1)
        pick = place == jnp.arange(wide * SLOTS)[:, None]
        pick = pick.astype(BF16)
        sent = jnp.dot(pick, features, preferred_element_type=F32).astype(BF16)
        rows = exchange(sent.reshape(wide, SLOTS, width))
        mine = place == (me * SLOTS + jnp.arange(SLOTS))[:, None]
        which = jnp.sum(jnp.where(mine, local + 1, 0), axis=1) - 1
        mask = (which[:, None] == jnp.arange(2 * held * rank) // rank).astype(F32)
        value = exchange(owner(rows, mask, shrink0, shrink1, expand0, expand1))
        return lax.dot_general(
            pick, value.reshape(wide * SLOTS, width), (((0,), (0,)), ((), ())), preferred_element_type=F32
        )

    adapter_out = round_of(0)

    weight1 = swap(base_weight)
    edge = block.shape[0] // 2
    blocks, whole, sources = [], [], []

    def add(source, *parts):
        whole.append(len(blocks))
        sources.append(source)
        blocks.extend(parts)

    shifts = list(range(chips // 4))
    columns = [block if k == 0 else move(block, shift(k)) for k in shifts]
    for k, column in zip(shifts, columns):
        source = (chip - 4 * k) % chips
        along_x = move(column, flip(1))
        along_y = move(column, flip(2))
        far0 = move(along_x[:edge], flip(2))
        far1 = move(along_y[edge:], flip(1))
        add(source, column)
        add(source ^ 1, along_x)
        add(source ^ 2, along_y)
        add(source ^ 3, far0, far1)
    places = jnp.stack([(2 * s + (core + side) % 2) * width for s in sources for side in range(2)])
    out0, out1 = base(places.astype(jnp.int32), blocks, tuple(whole), base_weight, weight1)
    got = swap(out1)

    rounds = (jnp.max(order) + per_chip) // per_chip
    if groups > 1:
        rounds = lax.pmax(rounds, "groups")
    _, adapter_out = lax.while_loop(
        lambda state: state[0] < rounds,
        lambda state: (state[0] + 1, state[1] + round_of(state[0])),
        (jnp.int32(1), adapter_out),
    )

    shape = (steps, half, width)
    a, b = out0.reshape(shape), got.reshape(shape)
    base_out = jnp.where(core == 0, jnp.stack([a, b], 1), jnp.stack([b, a], 1))
    result = base_out.reshape(count, width) + 2.0 * adapter_out
    return result.astype(BF16).reshape(steps, requests, width)


def solution(mesh):
    return jax.shard_map(
        functools.partial(body, mesh.shape["groups"]),
        mesh=mesh,
        in_specs=(
            P(None, "groups", "wide"),
            P("wide", None),
            P("wide", None, None),
            P("wide", None, None),
            P(),
            P(None, "groups"),
        ),
        out_specs=P(None, "groups", "wide"),
        check_vma=False,
    )
```

```python
import functools

import jax
import jax.numpy as jnp
from jax import lax
from jax.experimental import pallas as pl
from jax.experimental.pallas import tpu as pltpu
from jax.sharding import PartitionSpec as P

SLOTS = 32
LIMIT = 40 << 20
NT = (((1,), (1,)), ((), ()))
F32 = jnp.float32
BF16 = jnp.bfloat16
HBM = pl.BlockSpec(memory_space=pl.ANY)
VMEM = pl.BlockSpec(memory_space=pltpu.VMEM)
SMEM = pl.BlockSpec(memory_space=pltpu.SMEM)


def take(place_ref, blocks, tables, totals, packed=None):
    rows = totals[0].shape[0]
    for part, block in enumerate(blocks):
        if packed is not None:
            packed[part * rows : (part + 1) * rows, :] = block
        width = block.shape[1]
        columns = pl.ds(pl.multiple_of(place_ref[part], width), width)
        totals = [
            total + lax.dot_general(block, table[:, columns], NT, preferred_element_type=F32)
            for total, table in zip(totals, tables)
        ]
    return totals


def parts_of(refs, whole, rows):
    parts = []
    for index in whole:
        part = refs[index][...]
        if part.shape[0] != rows:
            part = jnp.concatenate([part, refs[index + 1][...]], axis=0)
        parts.append(part)
    return parts


def first_kernel(whole, place_ref, *refs):
    *blocks, t0_ref, t1_ref, out0_ref, out1_ref, packed_ref = refs
    parts = parts_of(blocks, whole, out0_ref.shape[0])
    totals = [jnp.zeros(out0_ref.shape, F32), jnp.zeros(out1_ref.shape, F32)]
    out0_ref[...], out1_ref[...] = take(place_ref, parts, (t0_ref, t1_ref), totals, packed_ref)


def first(places, blocks, whole, tables):
    rows, width = blocks[0].shape
    shape = jax.ShapeDtypeStruct((rows, tables[0].shape[0]), F32)
    return pl.pallas_call(
        functools.partial(first_kernel, whole),
        out_shape=(shape, shape, jax.ShapeDtypeStruct((len(whole) * rows, width), BF16)),
        in_specs=[SMEM] + [VMEM] * (len(blocks) + 2),
        out_specs=(VMEM,) * 3,
        compiler_params=pltpu.CompilerParams(vmem_limit_bytes=LIMIT),
        name="first",
    )(places, *blocks, *tables)


def base_kernel(place_ref, *refs):
    *packs, table_ref, out_ref = refs
    rows = out_ref.shape[0]
    parts = [pack[start : start + rows, :] for pack in packs for start in range(0, pack.shape[0], rows)]
    (out_ref[...],) = take(place_ref, parts, (table_ref,), [jnp.zeros(out_ref.shape, F32)])


def base(places, packs, table, rows, name):
    return pl.pallas_call(
        base_kernel,
        out_shape=jax.ShapeDtypeStruct((rows, table.shape[0]), F32),
        in_specs=[SMEM] + [VMEM] * (len(packs) + 1),
        out_specs=VMEM,
        compiler_params=pltpu.CompilerParams(vmem_limit_bytes=LIMIT),
        name=name,
    )(places, *packs, table)


def expand_rows(pick, lows, tables, out_ref):
    lows = [jnp.dot(pick, low, preferred_element_type=F32).astype(BF16) for low in lows]
    width = out_ref.shape[2]
    for part in range(out_ref.shape[0]):
        columns = slice(part * width, (part + 1) * width)
        value = jnp.dot(lows[0], tables[0][:, columns], preferred_element_type=F32)
        value += jnp.dot(lows[1], tables[1][:, columns], preferred_element_type=F32)
        out_ref[part] = value.astype(BF16)


def owner_kernel(whole, place_ref, *refs):
    *blocks, a0_ref, a1_ref, mask_ref, pick_ref, s0_ref, s1_ref, e0_ref, e1_ref = refs[:-5]
    out_ref, low_ref, packed_ref, given, sem = refs[-5:]
    rows, half = a0_ref.shape
    parts = parts_of(blocks, whole, rows)
    totals = take(place_ref, parts, (s0_ref, s1_ref), [a0_ref[...], a1_ref[...]], packed_ref)
    lows = []
    for side, total in enumerate(totals):
        columns = slice(side * half, (side + 1) * half)
        lows.append((total * mask_ref[:, columns]).astype(BF16))
        low_ref[:, columns] = lows[side]
    expand_rows(pick_ref[...], lows, (e0_ref, e1_ref), given)
    copy = pltpu.make_async_copy(given, out_ref, sem)
    copy.start()
    copy.wait()


def owner(places, blocks, whole, before, mask, pick, tables, out_shape):
    rows, width = mask.shape[0], blocks[-1].shape[1]
    return pl.pallas_call(
        functools.partial(owner_kernel, whole),
        out_shape=(
            jax.ShapeDtypeStruct(out_shape, BF16),
            jax.ShapeDtypeStruct(mask.shape, BF16),
            jax.ShapeDtypeStruct((len(whole) * rows, width), BF16),
        ),
        in_specs=[SMEM] + [VMEM] * (len(blocks) + 8),
        out_specs=(HBM, VMEM, VMEM),
        scratch_shapes=[pltpu.VMEM(out_shape, BF16), pltpu.SemaphoreType.DMA],
        compiler_params=pltpu.CompilerParams(vmem_limit_bytes=LIMIT),
        name="owner",
    )(places, *blocks, *before, mask, pick, *tables)


def again_kernel(pick_ref, low_ref, e0_ref, e1_ref, out_ref):
    half = e0_ref.shape[0]
    lows = [low_ref[:, :half], low_ref[:, half:]]
    expand_rows(pick_ref[...], lows, (e0_ref, e1_ref), out_ref)


def again(pick, low, e0, e1, out_shape):
    return pl.pallas_call(
        again_kernel,
        out_shape=jax.ShapeDtypeStruct(out_shape, BF16),
        in_specs=[VMEM] * 4,
        out_specs=VMEM,
        compiler_params=pltpu.CompilerParams(vmem_limit_bytes=LIMIT),
        name="again",
    )(pick, low, e0, e1)


def body(groups, inputs, base_weight, shrink_table, expand_table, table_slot, adapter_ids):
    wide = lax.axis_size("wide")
    me = lax.axis_index("wide")
    core, chip = me % 2, me // 2
    chips = wide // 2
    steps, requests, width = inputs.shape
    count = steps * requests
    held, rank, _ = shrink_table.shape

    def move(value, target):
        pairs = [(2 * c + k, 2 * target(c) + k) for c in range(chips) for k in range(2)]
        return lax.ppermute(value, "wide", pairs)

    def swap(value):
        return lax.ppermute(value, "wide", [(i, i ^ 1) for i in range(wide)])

    def after(value, *done):
        return lax.optimization_barrier((value, *done))[0]

    def flip(bits):
        return lambda c: c ^ bits

    def shift(k):
        return lambda c: (c + 4 * k) % chips

    half = requests // 2
    rows = steps * half
    split = inputs.reshape(steps, 2, half, width)
    own_half = lax.dynamic_index_in_dim(split, core, 1, keepdims=False).reshape(rows, width)
    other_half = lax.dynamic_index_in_dim(split, 1 - core, 1, keepdims=False).reshape(rows, width)
    got_half = swap(other_half)
    block = jnp.where(
        core == 0,
        jnp.concatenate([own_half, got_half], axis=1),
        jnp.concatenate([got_half, own_half], axis=1),
    )

    shrink0 = shrink_table.reshape(held * rank, -1)
    expand0 = expand_table.reshape(held * rank, -1)
    shrink1, expand1 = swap(after(shrink0, block)), swap(after(expand0, block))

    depth = chips // 4
    shifts = [0] + sorted(range(1, depth), key=lambda k: min(k, depth - k))
    edge = rows // 2
    x, y, far, z = {}, {}, {}, {0: block}

    def gather(some):
        blocks, whole, sources = [], [], []
        for k, bits in some:
            parts = far[k] if bits == 3 else ((z, x, y)[bits][k],)
            whole.append(len(blocks))
            sources.append(((chip - 4 * k) % chips) ^ bits)
            blocks.extend(parts)
        return (jnp.stack(sources) * (2 * width)).astype(jnp.int32), blocks, tuple(whole)

    x[0], y[0] = move(block, flip(1)), move(block, flip(2))
    for k in sorted(shifts[1:]):
        if k == 1:
            source = block
        elif k == depth - 1:
            source = after(block, shrink1, expand1)
        else:
            source = z[k - 1]
        z[k] = move(source, shift(k if k == depth - 1 else 1))
    far[0] = (move(after(x[0], y[0]), flip(2)),)
    for number, k in enumerate(shifts[1:], 1):
        ready = z[k]
        if number == 1:
            ready = after(ready, x[0], y[0])
        if number == depth - 1:
            ready = after(ready, far[0][0], x[1])
        x[k], y[k] = move(ready, flip(1)), move(ready, flip(2))
        if number < depth - 1:
            far[k] = (move(x[k], flip(2)) if number % 2 == 0 else move(y[k], flip(1)),)
    last = shifts[-1]
    early = [(k, bits) for k in shifts[:-3] for bits in range(4)] + [(shifts[-3], bits) for bits in range(3)]
    *sums, packed0 = first(*gather(early), (shrink0, shrink1))
    far[last] = (
        move(x[last][:edge], flip(2)),
        move(y[last][edge:], flip(1)),
    )
    tail = [(shifts[-3], 3)] + [(k, bits) for k in shifts[-2:] for bits in range(4)]

    table = table_slot.shape[0]
    ids = adapter_ids.reshape(count)
    slot = jnp.sum((ids[:, None] == jnp.arange(table, dtype=jnp.int32)) * table_slot, axis=1)
    side = jnp.arange(count) % requests // half
    holder = slot // (2 * held) * 2 + side
    earlier = jnp.arange(count)[:, None] > jnp.arange(count)
    order = jnp.sum((holder[:, None] == holder) & earlier, axis=1)
    here = lax.dynamic_index_in_dim(
        jnp.stack([slot, holder, order]).reshape(3, steps, 2, half), core, 2, keepdims=False
    ).reshape(3, rows)
    local = (here[0] - core * held) % (2 * held)
    mask = (local[:, None] == jnp.arange(2 * held * rank) // rank).astype(F32)
    chosen = jnp.where(here[1] == me, here[2], -1)

    def pick_of(index):
        return (chosen == (index * SLOTS + jnp.arange(SLOTS))[:, None]).astype(BF16)

    def give_back(sent, index):
        value = lax.all_to_all(sent, "wide", split_axis=0, concat_axis=0, tiled=True)
        rest = order - index * SLOTS
        place = jnp.where((rest >= 0) & (rest < SLOTS), holder * SLOTS + rest, -1)
        spread = (place[:, None] == jnp.arange(wide * SLOTS)).astype(BF16)
        return jnp.dot(spread, value.reshape(wide * SLOTS, width), preferred_element_type=F32)

    out_shape = (wide, SLOTS, width)
    sent, low, packed1 = owner(
        *gather(tail), sums, mask, pick_of(0), (shrink0, shrink1, expand0, expand1), out_shape
    )
    adapter_out = give_back(sent, 0)
    weight1 = swap(after(base_weight, low))
    places = gather(early + tail)[0]
    out0 = base(places, (packed0, packed1), base_weight, rows, "base")
    out1 = base(places, (packed0, packed1), weight1, rows, "other")
    got = swap(out1)

    rounds = jnp.max(order) // SLOTS + 1
    if groups > 1:
        rounds = lax.pmax(rounds, "groups")
    _, adapter_out = lax.while_loop(
        lambda state: state[0] < rounds,
        lambda state: (
            state[0] + 1,
            state[1] + give_back(again(pick_of(state[0]), low, expand0, expand1, out_shape), state[0]),
        ),
        (jnp.int32(1), adapter_out),
    )

    shape = (steps, half, width)
    a, b = out0.reshape(shape), got.reshape(shape)
    base_out = jnp.where(core == 0, jnp.stack([a, b], 1), jnp.stack([b, a], 1))
    result = base_out.reshape(count, width) + 2.0 * adapter_out
    return result.astype(BF16).reshape(steps, requests, width)


def solution(mesh):
    return jax.shard_map(
        functools.partial(body, mesh.shape["groups"]),
        mesh=mesh,
        in_specs=(
            P(None, "groups", "wide"),
            P("wide", None),
            P("wide", None, None),
            P("wide", None, None),
            P(),
            P(None, "groups"),
        ),
        out_specs=P(None, "groups", "wide"),
        check_vma=False,
    )
```

```python
import functools

import jax
import jax.numpy as jnp
from jax import lax
from jax.experimental import pallas as pl
from jax.experimental.pallas import tpu as pltpu
from jax.sharding import PartitionSpec as P

SLOTS = 32
LIMIT = 40 << 20
NT = (((1,), (1,)), ((), ()))
F32 = jnp.float32
BF16 = jnp.bfloat16
HBM = pl.BlockSpec(memory_space=pltpu.HBM)
VMEM = pl.BlockSpec(memory_space=pltpu.VMEM)
SMEM = pl.BlockSpec(memory_space=pltpu.SMEM)


def take(place_ref, blocks, tables, totals, packed=None):
    rows = totals[0].shape[0]
    for part, block in enumerate(blocks):
        if packed is not None:
            packed[part * rows : (part + 1) * rows, :] = block
        width = block.shape[1]
        columns = pl.ds(pl.multiple_of(place_ref[part], width), width)
        totals = [
            total + lax.dot_general(block, table[:, columns], NT, preferred_element_type=F32)
            for total, table in zip(totals, tables)
        ]
    return totals


def parts_of(refs, whole, rows):
    parts = []
    for index in whole:
        part = refs[index][...]
        if part.shape[0] != rows:
            part = jnp.concatenate([part, refs[index + 1][...]], axis=0)
        parts.append(part)
    return parts


def first_kernel(whole, place_ref, *refs):
    *blocks, s0_ref, s1_ref, e1_ref = refs[:-6]
    out0_ref, out1_ref, packed_ref, s1v_ref, e1v_ref, sems = refs[-6:]
    copies = [
        pltpu.make_async_copy(s1_ref, s1v_ref, sems.at[0]),
        pltpu.make_async_copy(e1_ref, e1v_ref, sems.at[1]),
    ]
    for copy in copies:
        copy.start()
    parts = parts_of(blocks, whole, out0_ref.shape[0])
    (out0_ref[...],) = take(place_ref, parts, (s0_ref,), [jnp.zeros(out0_ref.shape, F32)], packed_ref)
    copies[0].wait()
    (out1_ref[...],) = take(place_ref, parts, (s1v_ref,), [jnp.zeros(out1_ref.shape, F32)])
    copies[1].wait()


def first(places, blocks, whole, s0, s1, e1):
    rows, width = blocks[0].shape
    shape = jax.ShapeDtypeStruct((rows, s0.shape[0]), F32)
    return pl.pallas_call(
        functools.partial(first_kernel, whole),
        out_shape=(
            shape,
            shape,
            jax.ShapeDtypeStruct((len(whole) * rows, width), BF16),
            jax.ShapeDtypeStruct(s1.shape, BF16),
            jax.ShapeDtypeStruct(e1.shape, BF16),
        ),
        in_specs=[SMEM] + [VMEM] * (len(blocks) + 1) + [HBM] * 2,
        out_specs=(VMEM,) * 5,
        scratch_shapes=[pltpu.SemaphoreType.DMA((2,))],
        compiler_params=pltpu.CompilerParams(vmem_limit_bytes=LIMIT),
        name="first",
    )(places, *blocks, s0, s1, e1)


def base_kernel(place_ref, *refs):
    *packs, table_ref, out_ref = refs
    rows = out_ref.shape[0]
    parts = [pack[start : start + rows, :] for pack in packs for start in range(0, pack.shape[0], rows)]
    (out_ref[...],) = take(place_ref, parts, (table_ref,), [jnp.zeros(out_ref.shape, F32)])


def base(places, packs, table, rows, name):
    return pl.pallas_call(
        base_kernel,
        out_shape=jax.ShapeDtypeStruct((rows, table.shape[0]), F32),
        in_specs=[SMEM] + [VMEM] * (len(packs) + 1),
        out_specs=VMEM,
        compiler_params=pltpu.CompilerParams(vmem_limit_bytes=LIMIT),
        name=name,
    )(places, *packs, table)


def expand_rows(pick, low, table, out_ref):
    low = jnp.dot(pick, low, preferred_element_type=F32).astype(BF16)
    width = out_ref.shape[2]
    for part in range(out_ref.shape[0]):
        columns = slice(part * width, (part + 1) * width)
        out_ref[part] = jnp.dot(low, table[:, columns], preferred_element_type=F32).astype(BF16)


def owner_kernel(whole, place_ref, *refs):
    *blocks, a0_ref, a1_ref, mask_ref, s0_ref, s1_ref, low_ref, packed_ref = refs
    rows, half = a0_ref.shape
    parts = parts_of(blocks, whole, rows)
    totals = take(place_ref, parts, (s0_ref, s1_ref), [a0_ref[...], a1_ref[...]], packed_ref)
    for side, total in enumerate(totals):
        columns = slice(side * half, (side + 1) * half)
        low_ref[:, columns] = (total * mask_ref[:, columns]).astype(BF16)


def owner(places, blocks, whole, before, mask, s0, s1):
    rows, width = mask.shape[0], blocks[-1].shape[1]
    return pl.pallas_call(
        functools.partial(owner_kernel, whole),
        out_shape=(
            jax.ShapeDtypeStruct(mask.shape, BF16),
            jax.ShapeDtypeStruct((len(whole) * rows, width), BF16),
        ),
        in_specs=[SMEM] + [VMEM] * (len(blocks) + 5),
        out_specs=(VMEM,) * 2,
        compiler_params=pltpu.CompilerParams(vmem_limit_bytes=LIMIT),
        name="owner",
    )(places, *blocks, *before, mask, s0, s1)


def again_kernel(pick_ref, low_ref, e0_ref, e1_ref, out_ref):
    expand_rows(pick_ref[...], low_ref[...], jnp.concatenate([e0_ref[...], e1_ref[...]], axis=0), out_ref)


def again(pick, low, e0, e1, out_shape):
    return pl.pallas_call(
        again_kernel,
        out_shape=jax.ShapeDtypeStruct(out_shape, BF16),
        in_specs=[VMEM] * 4,
        out_specs=VMEM,
        compiler_params=pltpu.CompilerParams(vmem_limit_bytes=LIMIT),
        name="again",
    )(pick, low, e0, e1)


def last_kernel(core_ref, place_ref, value_ref, own_ref, got_ref, extra_ref, out_ref):
    count, (slots, width) = place_ref.shape[0], value_ref.shape
    chunk = min(slots, 512)
    total = extra_ref[...]
    for start in range(0, slots, chunk):
        number = lax.broadcasted_iota(jnp.int32, (count, chunk), 1) + start
        spread = jnp.where(number == place_ref[...], 1.0, 0.0).astype(BF16)
        total += jnp.dot(spread, value_ref[start : start + chunk, :], preferred_element_type=F32)
    steps, _, half, _ = out_ref.shape
    for step in range(steps):
        own = own_ref[step * half : (step + 1) * half, :]
        got = got_ref[step * half : (step + 1) * half, :]
        for side in range(2):
            row = (2 * step + side) * half
            base_out = jnp.where(core_ref[0] == side, own, got)
            out_ref[step, side] = (base_out + 2.0 * total[row : row + half, :]).astype(BF16)


def finish(core, place, value, own, got, extra, shape):
    return pl.pallas_call(
        last_kernel,
        out_shape=jax.ShapeDtypeStruct(shape, BF16),
        in_specs=[SMEM] + [VMEM] * 5,
        out_specs=VMEM,
        compiler_params=pltpu.CompilerParams(vmem_limit_bytes=LIMIT),
        name="finish",
    )(core, place, value, own, got, extra)


def body(groups, inputs, base_weight, shrink_table, expand_table, table_slot, adapter_ids):
    wide = lax.axis_size("wide")
    me = lax.axis_index("wide")
    core, chip = me % 2, me // 2
    chips = wide // 2
    steps, requests, width = inputs.shape
    count = steps * requests
    held, rank, _ = shrink_table.shape

    def move(value, target):
        pairs = [(2 * c + k, 2 * target(c) + k) for c in range(chips) for k in range(2)]
        return lax.ppermute(value, "wide", pairs)

    def swap(value):
        return lax.ppermute(value, "wide", [(i, i ^ 1) for i in range(wide)])

    def after(value, *done):
        return lax.optimization_barrier((value, *done))[0]

    def flip(bits):
        return lambda c: c ^ bits

    def shift(k):
        return lambda c: (c + 4 * k) % chips

    half = requests // 2
    rows = steps * half
    split = inputs.reshape(steps, 2, half, width)
    own_half = lax.dynamic_index_in_dim(split, core, 1, keepdims=False).reshape(rows, width)
    other_half = lax.dynamic_index_in_dim(split, 1 - core, 1, keepdims=False).reshape(rows, width)
    got_half = swap(other_half)
    block = jnp.where(
        core == 0,
        jnp.concatenate([own_half, got_half], axis=1),
        jnp.concatenate([got_half, own_half], axis=1),
    )

    shrink0 = shrink_table.reshape(held * rank, -1)
    expand0 = expand_table.reshape(held * rank, -1)
    shrink1, expand1 = swap(after(shrink0, block)), swap(after(expand0, block))

    depth = chips // 4
    shifts = [0] + sorted(range(1, depth), key=lambda k: min(k, depth - k))
    edge = rows // 2
    x, y, far, z = {}, {}, {}, {0: block}

    def gather(some):
        blocks, whole, sources = [], [], []
        for k, bits in some:
            parts = far[k] if bits == 3 else ((z, x, y)[bits][k],)
            whole.append(len(blocks))
            sources.append(((chip - 4 * k) % chips) ^ bits)
            blocks.extend(parts)
        return (jnp.stack(sources) * (2 * width)).astype(jnp.int32), blocks, tuple(whole)

    x[0], y[0] = move(block, flip(1)), move(block, flip(2))
    for k in sorted(shifts[1:]):
        if k == 1:
            source = block
        elif k == depth - 1:
            source = after(block, shrink1, expand1)
        else:
            source = z[k - 1]
        z[k] = move(source, shift(k if k == depth - 1 else 1))
    far[0] = (move(after(x[0], y[0]), flip(2)),)
    for number, k in enumerate(shifts[1:], 1):
        ready = z[k]
        if number == 1:
            ready = after(ready, x[0], y[0])
        if number == depth - 1:
            ready = after(ready, far[0][0], x[1])
        x[k], y[k] = move(ready, flip(1)), move(ready, flip(2))
        if number < depth - 1:
            far[k] = (move(x[k], flip(2)) if number % 2 == 0 else move(y[k], flip(1)),)
    last = shifts[-1]
    early = [(k, bits) for k in shifts[:-3] for bits in range(4)] + [(shifts[-3], bits) for bits in range(3)]
    *sums, packed0, near_shrink, near_expand = first(*gather(early), shrink0, shrink1, expand1)
    far[last] = (
        move(x[last][:edge], flip(2)),
        move(y[last][edge:], flip(1)),
    )
    tail = [(shifts[-3], 3)] + [(k, bits) for k in shifts[-2:] for bits in range(4)]

    table = table_slot.shape[0]
    ids = adapter_ids.reshape(count)
    slot = jnp.sum((ids[:, None] == jnp.arange(table, dtype=jnp.int32)) * table_slot, axis=1)
    side = jnp.arange(count) % requests // half
    holder = slot // (2 * held) * 2 + side
    earlier = jnp.arange(count)[:, None] > jnp.arange(count)
    order = jnp.sum((holder[:, None] == holder) & earlier, axis=1)
    here = lax.dynamic_index_in_dim(
        jnp.stack([slot, holder, order]).reshape(3, steps, 2, half), core, 2, keepdims=False
    ).reshape(3, rows)
    local = (here[0] - core * held) % (2 * held)
    mask = (local[:, None] == jnp.arange(2 * held * rank) // rank).astype(F32)
    chosen = jnp.where(here[1] == me, here[2], -1)

    def pick_of(index):
        return (chosen == (index * SLOTS + jnp.arange(SLOTS))[:, None]).astype(BF16)

    def give_back(sent):
        value = lax.all_to_all(sent, "wide", split_axis=0, concat_axis=0, tiled=True)
        return value.reshape(wide * SLOTS, width)

    def place_of(index):
        rest = order - index * SLOTS
        return jnp.where((rest >= 0) & (rest < SLOTS), holder * SLOTS + rest, -1)[:, None]

    out_shape = (wide, SLOTS, width)
    low, packed1 = owner(*gather(tail), sums, mask, shrink0, near_shrink)
    sent = again(pick_of(0), low, expand0, near_expand, out_shape)
    value = give_back(sent)
    weight1 = swap(after(base_weight, sent))
    places = gather(early + tail)[0]
    out1 = base(places, (packed0, packed1), weight1, rows, "other")
    out0 = base(after(places, out1), (packed0, packed1), base_weight, rows, "base")
    got = swap(out1)

    rounds = jnp.max(order) // SLOTS + 1
    if groups > 1:
        rounds = lax.pmax(rounds, "groups")

    def more(state):
        index, total = state
        got_rows = give_back(again(pick_of(index), low, expand0, expand1, out_shape))
        spread = (place_of(index) == jnp.arange(wide * SLOTS)).astype(BF16)
        return index + 1, total + jnp.dot(spread, got_rows, preferred_element_type=F32)

    _, extra = lax.while_loop(
        lambda state: state[0] < rounds, more, (after(jnp.int32(1), value, got, out0), jnp.zeros((count, width), F32))
    )

    result = finish(
        core.astype(jnp.int32)[None], place_of(0), value, out0, got, extra, (steps, 2, half, width)
    )
    return result.reshape(steps, requests, width)


def solution(mesh):
    return jax.shard_map(
        functools.partial(body, mesh.shape["groups"]),
        mesh=mesh,
        in_specs=(
            P(None, "groups", "wide"),
            P("wide", None),
            P("wide", None, None),
            P("wide", None, None),
            P(),
            P(None, "groups"),
        ),
        out_specs=P(None, "groups", "wide"),
        check_vma=False,
    )
```

```python
import functools

import jax
import jax.numpy as jnp
from jax import lax
from jax.experimental import pallas as pl
from jax.experimental.pallas import tpu as pltpu
from jax.sharding import PartitionSpec as P

SLOTS = 32
LIMIT = 40 << 20
NT = (((1,), (1,)), ((), ()))
F32 = jnp.float32
BF16 = jnp.bfloat16
HBM = pl.BlockSpec(memory_space=pltpu.HBM)
VMEM = pl.BlockSpec(memory_space=pltpu.VMEM)
SMEM = pl.BlockSpec(memory_space=pltpu.SMEM)


def take(place_ref, blocks, tables, totals, packed=None):
    rows = totals[0].shape[0]
    for part, block in enumerate(blocks):
        if packed is not None:
            packed[part * rows : (part + 1) * rows, :] = block
        width = block.shape[1]
        columns = pl.ds(pl.multiple_of(place_ref[part], width), width)
        totals = [
            total + lax.dot_general(block, table[:, columns], NT, preferred_element_type=F32)
            for total, table in zip(totals, tables)
        ]
    return totals


def parts_of(refs, whole, rows):
    parts = []
    for index in whole:
        part = refs[index][...]
        if part.shape[0] != rows:
            part = jnp.concatenate([part, refs[index + 1][...]], axis=0)
        parts.append(part)
    return parts


def first_kernel(whole, place_ref, *refs):
    *blocks, s0_ref, s1_ref, e1_ref = refs[:-6]
    out0_ref, out1_ref, packed_ref, s1v_ref, e1v_ref, sems = refs[-6:]
    copies = [
        pltpu.make_async_copy(s1_ref, s1v_ref, sems.at[0]),
        pltpu.make_async_copy(e1_ref, e1v_ref, sems.at[1]),
    ]
    for copy in copies:
        copy.start()
    parts = parts_of(blocks, whole, out0_ref.shape[0])
    (out0_ref[...],) = take(place_ref, parts, (s0_ref,), [jnp.zeros(out0_ref.shape, F32)], packed_ref)
    copies[0].wait()
    (out1_ref[...],) = take(place_ref, parts, (s1v_ref,), [jnp.zeros(out1_ref.shape, F32)])
    copies[1].wait()


def first(places, blocks, whole, s0, s1, e1):
    rows, width = blocks[0].shape
    shape = jax.ShapeDtypeStruct((rows, s0.shape[0]), F32)
    return pl.pallas_call(
        functools.partial(first_kernel, whole),
        out_shape=(
            shape,
            shape,
            jax.ShapeDtypeStruct((len(whole) * rows, width), BF16),
            jax.ShapeDtypeStruct(s1.shape, BF16),
            jax.ShapeDtypeStruct(e1.shape, BF16),
        ),
        in_specs=[SMEM] + [VMEM] * (len(blocks) + 1) + [HBM] * 2,
        out_specs=(VMEM,) * 5,
        scratch_shapes=[pltpu.SemaphoreType.DMA((2,))],
        compiler_params=pltpu.CompilerParams(vmem_limit_bytes=LIMIT),
        name="first",
    )(places, *blocks, s0, s1, e1)


def base_kernel(place_ref, *refs):
    *packs, table_ref, out_ref = refs
    rows = out_ref.shape[0]
    parts = [pack[start : start + rows, :] for pack in packs for start in range(0, pack.shape[0], rows)]
    (out_ref[...],) = take(place_ref, parts, (table_ref,), [jnp.zeros(out_ref.shape, F32)])


def base(places, packs, table, rows, name):
    return pl.pallas_call(
        base_kernel,
        out_shape=jax.ShapeDtypeStruct((rows, table.shape[0]), F32),
        in_specs=[SMEM] + [VMEM] * (len(packs) + 1),
        out_specs=VMEM,
        compiler_params=pltpu.CompilerParams(vmem_limit_bytes=LIMIT),
        name=name,
    )(places, *packs, table)


def expand_rows(pick, low, table, out_ref):
    low = jnp.dot(pick, low, preferred_element_type=F32).astype(BF16)
    width = out_ref.shape[2]
    for part in range(out_ref.shape[0]):
        columns = slice(part * width, (part + 1) * width)
        out_ref[part] = jnp.dot(low, table[:, columns], preferred_element_type=F32).astype(BF16)


def owner_kernel(whole, place_ref, *refs):
    *blocks, a0_ref, a1_ref, mask_ref, s0_ref, s1_ref, low_ref, packed_ref = refs
    rows, half = a0_ref.shape
    parts = parts_of(blocks, whole, rows)
    totals = take(place_ref, parts, (s0_ref, s1_ref), [a0_ref[...], a1_ref[...]], packed_ref)
    for side, total in enumerate(totals):
        columns = slice(side * half, (side + 1) * half)
        low_ref[:, columns] = (total * mask_ref[:, columns]).astype(BF16)


def owner(places, blocks, whole, before, mask, s0, s1):
    rows, width = mask.shape[0], blocks[-1].shape[1]
    return pl.pallas_call(
        functools.partial(owner_kernel, whole),
        out_shape=(
            jax.ShapeDtypeStruct(mask.shape, BF16),
            jax.ShapeDtypeStruct((len(whole) * rows, width), BF16),
        ),
        in_specs=[SMEM] + [VMEM] * (len(blocks) + 5),
        out_specs=(VMEM,) * 2,
        compiler_params=pltpu.CompilerParams(vmem_limit_bytes=LIMIT),
        name="owner",
    )(places, *blocks, *before, mask, s0, s1)


def again_kernel(pick_ref, low_ref, e0_ref, e1_ref, out_ref):
    expand_rows(pick_ref[...], low_ref[...], jnp.concatenate([e0_ref[...], e1_ref[...]], axis=0), out_ref)


def again(pick, low, e0, e1, out_shape):
    return pl.pallas_call(
        again_kernel,
        out_shape=jax.ShapeDtypeStruct(out_shape, BF16),
        in_specs=[VMEM] * 4,
        out_specs=VMEM,
        compiler_params=pltpu.CompilerParams(vmem_limit_bytes=LIMIT),
        name="again",
    )(pick, low, e0, e1)


def last_kernel(core_ref, place_ref, value_ref, own_ref, got_ref, extra_ref, out_ref):
    count, (slots, width) = place_ref.shape[0], value_ref.shape
    chunk = min(slots, 512)
    total = extra_ref[...]
    for start in range(0, slots, chunk):
        number = lax.broadcasted_iota(jnp.int32, (count, chunk), 1) + start
        spread = jnp.where(number == place_ref[...], 1.0, 0.0).astype(BF16)
        total += jnp.dot(spread, value_ref[start : start + chunk, :], preferred_element_type=F32)
    steps, _, half, _ = out_ref.shape
    for step in range(steps):
        own = own_ref[step * half : (step + 1) * half, :]
        got = got_ref[step * half : (step + 1) * half, :]
        for side in range(2):
            row = (2 * step + side) * half
            base_out = jnp.where(core_ref[0] == side, own, got)
            out_ref[step, side] = (base_out + 2.0 * total[row : row + half, :]).astype(BF16)


def finish(core, place, value, own, got, extra, shape):
    return pl.pallas_call(
        last_kernel,
        out_shape=jax.ShapeDtypeStruct(shape, BF16),
        in_specs=[SMEM] + [VMEM] * 5,
        out_specs=VMEM,
        compiler_params=pltpu.CompilerParams(vmem_limit_bytes=LIMIT),
        name="finish",
    )(core, place, value, own, got, extra)


def body(groups, inputs, base_weight, shrink_table, expand_table, table_slot, adapter_ids):
    wide = lax.axis_size("wide")
    me = lax.axis_index("wide")
    core, chip = me % 2, me // 2
    chips = wide // 2
    steps, requests, width = inputs.shape
    count = steps * requests
    held, rank, _ = shrink_table.shape

    def move(value, target):
        pairs = [(2 * c + k, 2 * target(c) + k) for c in range(chips) for k in range(2)]
        return lax.ppermute(value, "wide", pairs)

    def swap(value):
        return lax.ppermute(value, "wide", [(i, i ^ 1) for i in range(wide)])

    def after(value, *done):
        return lax.optimization_barrier((value, *done))[0]

    def flip(bits):
        return lambda c: c ^ bits

    def shift(k):
        return lambda c: (c + 4 * k) % chips

    half = requests // 2
    rows = steps * half
    split = inputs.reshape(steps, 2, half, width)
    own_half = lax.dynamic_index_in_dim(split, core, 1, keepdims=False).reshape(rows, width)
    other_half = lax.dynamic_index_in_dim(split, 1 - core, 1, keepdims=False).reshape(rows, width)
    got_half = swap(other_half)
    block = jnp.where(
        core == 0,
        jnp.concatenate([own_half, got_half], axis=1),
        jnp.concatenate([got_half, own_half], axis=1),
    )

    shrink0 = shrink_table.reshape(held * rank, -1)
    expand0 = expand_table.reshape(held * rank, -1)
    shrink1, expand1 = swap(after(shrink0, block)), swap(after(expand0, block))

    depth = chips // 4
    shifts = [0] + sorted(range(1, depth), key=lambda k: min(k, depth - k))
    edge = rows // 2
    x, y, far, z = {}, {}, {}, {0: block}

    def gather(some):
        blocks, whole, sources = [], [], []
        for k, bits in some:
            parts = far[k] if bits == 3 else ((z, x, y)[bits][k],)
            whole.append(len(blocks))
            sources.append(((chip - 4 * k) % chips) ^ bits)
            blocks.extend(parts)
        return (jnp.stack(sources) * (2 * width)).astype(jnp.int32), blocks, tuple(whole)

    x[0], y[0] = move(block, flip(1)), move(block, flip(2))
    for k in sorted(shifts[1:]):
        if k == 1:
            source = block
        elif k == depth - 1:
            source = after(block, x[0], shrink1)
        else:
            source = z[k - 1]
        z[k] = move(source, shift(k if k == depth - 1 else 1))
    far[0] = (move(after(x[0], y[0], expand1), flip(2)),)
    for number, k in enumerate(shifts[1:], 1):
        ready = z[k]
        if number == 1:
            ready = after(ready, x[0], y[0])
        if number == depth - 1:
            ready = after(ready, far[0][0], x[1])
        x[k], y[k] = move(ready, flip(1)), move(ready, flip(2))
        if number < depth - 1:
            far[k] = (move(x[k], flip(2)) if number % 2 == 0 else move(y[k], flip(1)),)
    last = shifts[-1]
    early = [(k, bits) for k in shifts[:-3] for bits in range(4)] + [(shifts[-3], bits) for bits in range(3)]
    *sums, packed0, near_shrink, near_expand = first(*gather(early), shrink0, shrink1, expand1)
    far[last] = (
        move(x[last][:edge], flip(2)),
        move(y[last][edge:], flip(1)),
    )
    tail = [(shifts[-3], 3)] + [(k, bits) for k in shifts[-2:] for bits in range(4)]

    table = table_slot.shape[0]
    ids = adapter_ids.reshape(count)
    slot = jnp.sum((ids[:, None] == jnp.arange(table, dtype=jnp.int32)) * table_slot, axis=1)
    side = jnp.arange(count) % requests // half
    holder = slot // (2 * held) * 2 + side
    earlier = jnp.arange(count)[:, None] > jnp.arange(count)
    order = jnp.sum((holder[:, None] == holder) & earlier, axis=1)
    here = lax.dynamic_index_in_dim(
        jnp.stack([slot, holder, order]).reshape(3, steps, 2, half), core, 2, keepdims=False
    ).reshape(3, rows)
    local = (here[0] - core * held) % (2 * held)
    mask = (local[:, None] == jnp.arange(2 * held * rank) // rank).astype(F32)
    chosen = jnp.where(here[1] == me, here[2], -1)

    def pick_of(index):
        return (chosen == (index * SLOTS + jnp.arange(SLOTS))[:, None]).astype(BF16)

    def give_back(sent):
        value = lax.all_to_all(sent, "wide", split_axis=0, concat_axis=0, tiled=True)
        return value.reshape(wide * SLOTS, width)

    def place_of(index):
        rest = order - index * SLOTS
        return jnp.where((rest >= 0) & (rest < SLOTS), holder * SLOTS + rest, -1)[:, None]

    out_shape = (wide, SLOTS, width)
    low, packed1 = owner(*gather(tail), sums, mask, shrink0, near_shrink)
    sent = again(pick_of(0), low, expand0, near_expand, out_shape)
    value = give_back(sent)
    weight1 = swap(after(base_weight, sent))
    places = gather(early + tail)[0]
    out1 = base(places, (packed0, packed1), weight1, rows, "other")
    out0 = base(after(places, out1), (packed0, packed1), base_weight, rows, "base")
    got = swap(out1)

    rounds = jnp.max(order) // SLOTS + 1
    if groups > 1:
        rounds = lax.pmax(rounds, "groups")

    def more(state):
        index, total = state
        got_rows = give_back(again(pick_of(index), low, expand0, expand1, out_shape))
        spread = (place_of(index) == jnp.arange(wide * SLOTS)).astype(BF16)
        return index + 1, total + jnp.dot(spread, got_rows, preferred_element_type=F32)

    _, extra = lax.while_loop(
        lambda state: state[0] < rounds, more, (after(jnp.int32(1), value, got, out0), jnp.zeros((count, width), F32))
    )

    result = finish(
        core.astype(jnp.int32)[None], place_of(0), value, out0, got, extra, (steps, 2, half, width)
    )
    return result.reshape(steps, requests, width)


def solution(mesh):
    return jax.shard_map(
        functools.partial(body, mesh.shape["groups"]),
        mesh=mesh,
        in_specs=(
            P(None, "groups", "wide"),
            P("wide", None),
            P("wide", None, None),
            P("wide", None, None),
            P(),
            P(None, "groups"),
        ),
        out_specs=P(None, "groups", "wide"),
        check_vma=False,
    )
```

```python
import functools

import jax
import jax.numpy as jnp
from jax import lax
from jax.experimental import pallas as pl
from jax.experimental.pallas import tpu as pltpu
from jax.sharding import PartitionSpec as P

SLOTS = 32
LIMIT = 40 << 20
NT = (((1,), (1,)), ((), ()))
F32 = jnp.float32
BF16 = jnp.bfloat16
HBM = pl.BlockSpec(memory_space=pltpu.HBM)
VMEM = pl.BlockSpec(memory_space=pltpu.VMEM)
SMEM = pl.BlockSpec(memory_space=pltpu.SMEM)


def take(place_ref, blocks, tables, totals, packed=None):
    rows = totals[0].shape[0]
    for part, block in enumerate(blocks):
        if packed is not None:
            packed[part * rows : (part + 1) * rows, :] = block
        width = block.shape[1]
        columns = pl.ds(pl.multiple_of(place_ref[part], width), width)
        totals = [
            total + lax.dot_general(block, table[:, columns], NT, preferred_element_type=F32)
            for total, table in zip(totals, tables)
        ]
    return totals


def parts_of(refs, whole, rows):
    parts = []
    for index in whole:
        part = refs[index][...]
        if part.shape[0] != rows:
            part = jnp.concatenate([part, refs[index + 1][...]], axis=0)
        parts.append(part)
    return parts


def first_kernel(whole, place_ref, *refs):
    *blocks, s0_ref, s1_ref, e1_ref = refs[:-6]
    out0_ref, out1_ref, packed_ref, s1v_ref, e1v_ref, sems = refs[-6:]
    copies = [
        pltpu.make_async_copy(s1_ref, s1v_ref, sems.at[0]),
        pltpu.make_async_copy(e1_ref, e1v_ref, sems.at[1]),
    ]
    for copy in copies:
        copy.start()
    parts = parts_of(blocks, whole, out0_ref.shape[0])
    (out0_ref[...],) = take(place_ref, parts, (s0_ref,), [jnp.zeros(out0_ref.shape, F32)], packed_ref)
    copies[0].wait()
    (out1_ref[...],) = take(place_ref, parts, (s1v_ref,), [jnp.zeros(out1_ref.shape, F32)])
    copies[1].wait()


def first(places, blocks, whole, s0, s1, e1):
    rows, width = blocks[0].shape
    shape = jax.ShapeDtypeStruct((rows, s0.shape[0]), F32)
    return pl.pallas_call(
        functools.partial(first_kernel, whole),
        out_shape=(
            shape,
            shape,
            jax.ShapeDtypeStruct((len(whole) * rows, width), BF16),
            jax.ShapeDtypeStruct(s1.shape, BF16),
            jax.ShapeDtypeStruct(e1.shape, BF16),
        ),
        in_specs=[SMEM] + [VMEM] * (len(blocks) + 1) + [HBM] * 2,
        out_specs=(VMEM,) * 5,
        scratch_shapes=[pltpu.SemaphoreType.DMA((2,))],
        compiler_params=pltpu.CompilerParams(vmem_limit_bytes=LIMIT),
        name="first",
    )(places, *blocks, s0, s1, e1)


def base_kernel(place_ref, *refs):
    *packs, table_ref, out_ref = refs
    rows = out_ref.shape[0]
    parts = [pack[start : start + rows, :] for pack in packs for start in range(0, pack.shape[0], rows)]
    (out_ref[...],) = take(place_ref, parts, (table_ref,), [jnp.zeros(out_ref.shape, F32)])


def base(places, packs, table, rows, name):
    return pl.pallas_call(
        base_kernel,
        out_shape=jax.ShapeDtypeStruct((rows, table.shape[0]), F32),
        in_specs=[SMEM] + [VMEM] * (len(packs) + 1),
        out_specs=VMEM,
        compiler_params=pltpu.CompilerParams(vmem_limit_bytes=LIMIT),
        name=name,
    )(places, *packs, table)


def expand_rows(pick, low, table, out_ref):
    low = jnp.dot(pick, low, preferred_element_type=F32).astype(BF16)
    width = out_ref.shape[2]
    for part in range(out_ref.shape[0]):
        columns = slice(part * width, (part + 1) * width)
        out_ref[part] = jnp.dot(low, table[:, columns], preferred_element_type=F32).astype(BF16)


def owner_kernel(whole, place_ref, *refs):
    *blocks, a0_ref, a1_ref, mask_ref, s0_ref, s1_ref, low_ref, packed_ref = refs
    rows, half = a0_ref.shape
    parts = parts_of(blocks, whole, rows)
    totals = take(place_ref, parts, (s0_ref, s1_ref), [a0_ref[...], a1_ref[...]], packed_ref)
    for side, total in enumerate(totals):
        columns = slice(side * half, (side + 1) * half)
        low_ref[:, columns] = (total * mask_ref[:, columns]).astype(BF16)


def owner(places, blocks, whole, before, mask, s0, s1):
    rows, width = mask.shape[0], blocks[-1].shape[1]
    return pl.pallas_call(
        functools.partial(owner_kernel, whole),
        out_shape=(
            jax.ShapeDtypeStruct(mask.shape, BF16),
            jax.ShapeDtypeStruct((len(whole) * rows, width), BF16),
        ),
        in_specs=[SMEM] + [VMEM] * (len(blocks) + 5),
        out_specs=(VMEM,) * 2,
        compiler_params=pltpu.CompilerParams(vmem_limit_bytes=LIMIT),
        name="owner",
    )(places, *blocks, *before, mask, s0, s1)


def again_kernel(pick_ref, low_ref, e0_ref, e1_ref, out_ref):
    expand_rows(pick_ref[...], low_ref[...], jnp.concatenate([e0_ref[...], e1_ref[...]], axis=0), out_ref)


def again(pick, low, e0, e1, out_shape):
    return pl.pallas_call(
        again_kernel,
        out_shape=jax.ShapeDtypeStruct(out_shape, BF16),
        in_specs=[VMEM] * 4,
        out_specs=VMEM,
        compiler_params=pltpu.CompilerParams(vmem_limit_bytes=LIMIT),
        name="again",
    )(pick, low, e0, e1)


def last_kernel(core_ref, place_ref, value_ref, own_ref, got_ref, extra_ref, out_ref):
    count, (slots, width) = place_ref.shape[0], value_ref.shape
    chunk = min(slots, 512)
    total = extra_ref[...]
    for start in range(0, slots, chunk):
        number = lax.broadcasted_iota(jnp.int32, (count, chunk), 1) + start
        spread = jnp.where(number == place_ref[...], 1.0, 0.0).astype(BF16)
        total += jnp.dot(spread, value_ref[start : start + chunk, :], preferred_element_type=F32)
    steps, _, half, _ = out_ref.shape
    for step in range(steps):
        own = own_ref[step * half : (step + 1) * half, :]
        got = got_ref[step * half : (step + 1) * half, :]
        for side in range(2):
            row = (2 * step + side) * half
            base_out = jnp.where(core_ref[0] == side, own, got)
            out_ref[step, side] = (base_out + 2.0 * total[row : row + half, :]).astype(BF16)


def finish(core, place, value, own, got, extra, shape):
    return pl.pallas_call(
        last_kernel,
        out_shape=jax.ShapeDtypeStruct(shape, BF16),
        in_specs=[SMEM] + [VMEM] * 5,
        out_specs=VMEM,
        compiler_params=pltpu.CompilerParams(vmem_limit_bytes=LIMIT),
        name="finish",
    )(core, place, value, own, got, extra)


def body(groups, inputs, base_weight, shrink_table, expand_table, table_slot, adapter_ids):
    wide = lax.axis_size("wide")
    me = lax.axis_index("wide")
    core, chip = me % 2, me // 2
    chips = wide // 2
    steps, requests, width = inputs.shape
    count = steps * requests
    held, rank, _ = shrink_table.shape

    def move(value, target):
        pairs = [(2 * c + k, 2 * target(c) + k) for c in range(chips) for k in range(2)]
        return lax.ppermute(value, "wide", pairs)

    def swap(value):
        return lax.ppermute(value, "wide", [(i, i ^ 1) for i in range(wide)])

    def after(value, *done):
        return lax.optimization_barrier((value, *done))[0]

    def flip(bits):
        return lambda c: c ^ bits

    def shift(k):
        return lambda c: (c + 4 * k) % chips

    half = requests // 2
    rows = steps * half
    split = inputs.reshape(steps, 2, half, width)
    own_half = lax.dynamic_index_in_dim(split, core, 1, keepdims=False).reshape(rows, width)
    other_half = lax.dynamic_index_in_dim(split, 1 - core, 1, keepdims=False).reshape(rows, width)
    got_half = swap(other_half)
    block = jnp.where(
        core == 0,
        jnp.concatenate([own_half, got_half], axis=1),
        jnp.concatenate([got_half, own_half], axis=1),
    )

    shrink0 = shrink_table.reshape(held * rank, -1)
    expand0 = expand_table.reshape(held * rank, -1)
    shrink1, expand1 = swap(after(shrink0, block)), swap(after(expand0, block))

    depth = chips // 4
    shifts = [0] + sorted(range(1, depth), key=lambda k: min(k, depth - k))
    edge = rows // 2
    x, y, far, z = {}, {}, {}, {0: block}

    def gather(some):
        blocks, whole, sources = [], [], []
        for k, bits in some:
            parts = far[k] if bits == 3 else ((z, x, y)[bits][k],)
            whole.append(len(blocks))
            sources.append(((chip - 4 * k) % chips) ^ bits)
            blocks.extend(parts)
        return (jnp.stack(sources) * (2 * width)).astype(jnp.int32), blocks, tuple(whole)

    x[0], y[0] = move(block, flip(1)), move(block, flip(2))
    for k in sorted(shifts[1:]):
        if k == 1:
            source = block
        elif k == depth - 1:
            source = after(block, x[0], shrink1)
        else:
            source = z[k - 1]
        z[k] = move(source, shift(k if k == depth - 1 else 1))
    far[0] = (move(after(x[0], y[0], expand1), flip(2)),)
    for number, k in enumerate(shifts[1:], 1):
        ready = z[k]
        if number == 1:
            ready = after(ready, x[0], y[0])
        if number == depth - 1:
            ready = after(ready, far[0][0])
        x[k], y[k] = move(ready, flip(1)), move(ready, flip(2))
        if number < depth - 1:
            far[k] = (move(x[k], flip(2)) if number % 2 == 0 else move(y[k], flip(1)),)
    last = shifts[-1]
    early = [(k, bits) for k in shifts[:-3] for bits in range(4)] + [(shifts[-3], bits) for bits in range(3)]
    *sums, packed0, near_shrink, near_expand = first(*gather(early), shrink0, shrink1, expand1)
    far[last] = (
        move(x[last][:edge], flip(2)),
        move(y[last][edge:], flip(1)),
    )
    tail = [(shifts[-3], 3)] + [(k, bits) for k in shifts[-2:] for bits in range(4)]

    table = table_slot.shape[0]
    ids = adapter_ids.reshape(count)
    slot = jnp.sum((ids[:, None] == jnp.arange(table, dtype=jnp.int32)) * table_slot, axis=1)
    side = jnp.arange(count) % requests // half
    holder = slot // (2 * held) * 2 + side
    earlier = jnp.arange(count)[:, None] > jnp.arange(count)
    order = jnp.sum((holder[:, None] == holder) & earlier, axis=1)
    here = lax.dynamic_index_in_dim(
        jnp.stack([slot, holder, order]).reshape(3, steps, 2, half), core, 2, keepdims=False
    ).reshape(3, rows)
    local = (here[0] - core * held) % (2 * held)
    mask = (local[:, None] == jnp.arange(2 * held * rank) // rank).astype(F32)
    chosen = jnp.where(here[1] == me, here[2], -1)

    def pick_of(index):
        return (chosen == (index * SLOTS + jnp.arange(SLOTS))[:, None]).astype(BF16)

    def give_back(sent):
        value = lax.all_to_all(sent, "wide", split_axis=0, concat_axis=0, tiled=True)
        return value.reshape(wide * SLOTS, width)

    def place_of(index):
        rest = order - index * SLOTS
        return jnp.where((rest >= 0) & (rest < SLOTS), holder * SLOTS + rest, -1)[:, None]

    out_shape = (wide, SLOTS, width)
    low, packed1 = owner(*gather(tail), sums, mask, shrink0, near_shrink)
    sent = again(pick_of(0), low, expand0, near_expand, out_shape)
    value = give_back(sent)
    weight1 = swap(after(base_weight, sent))
    places = gather(early + tail)[0]
    out1 = base(places, (packed0, packed1), weight1, rows, "other")
    out0 = base(after(places, out1), (packed0, packed1), base_weight, rows, "base")
    got = swap(out1)

    rounds = jnp.max(order) // SLOTS + 1
    if groups > 1:
        rounds = lax.pmax(rounds, "groups")

    def more(state):
        index, total = state
        got_rows = give_back(again(pick_of(index), low, expand0, expand1, out_shape))
        spread = (place_of(index) == jnp.arange(wide * SLOTS)).astype(BF16)
        return index + 1, total + jnp.dot(spread, got_rows, preferred_element_type=F32)

    _, extra = lax.while_loop(
        lambda state: state[0] < rounds, more, (after(jnp.int32(1), value, got, out0), jnp.zeros((count, width), F32))
    )

    result = finish(
        core.astype(jnp.int32)[None], place_of(0), value, out0, got, extra, (steps, 2, half, width)
    )
    return result.reshape(steps, requests, width)


def solution(mesh):
    return jax.shard_map(
        functools.partial(body, mesh.shape["groups"]),
        mesh=mesh,
        in_specs=(
            P(None, "groups", "wide"),
            P("wide", None),
            P("wide", None, None),
            P("wide", None, None),
            P(),
            P(None, "groups"),
        ),
        out_specs=P(None, "groups", "wide"),
        check_vma=False,
    )
```
